32 devices in a mesh: front: 4 (over x, core), wide: 8 (over z, y).
Axes of the slice: x: 2, y: 2, z: 4, core: 2. Of those that a mesh axis runs over, the one named last changes fastest.
Arguments:
- inv_diag: bfloat16 [4, 8192, 8192], P('front', 'wide'), as said below
- below: bfloat16 [4, 6144, 8192], P('front', 'wide'), may hold values from -0.0625 to 0.0625
- rhs: bfloat16 [4, 8192, 256], P('front', 'wide'), may hold values from -6 to 6
- tile_count: int32 [4], replicated, may hold values from 36 to 48, as said below
- tile_owner: int32 [4, 48, 1], P('front', 'wide'), may hold values from 0 to 3; in each aligned block of 6 rows (0 to 5, 6 to 11, ..., all dimensions but the last counted through in order) at most 2 rows name the same one
- tile_rows: int32 [4, 48, 128], P('front', 'wide'), may hold values from 0 to 511
- parent_rhs: bfloat16 [4, 4096, 256], P('front', 'wide'), may hold values from -6 to 6
Outputs:
- solved: bfloat16 [4, 8192, 256], P('front', 'wide')
- parent_new: float32 [4, 4096, 256], P('front', 'wide')
The draws below stay inside these ranges and needn't reach their ends.
Inputs may be any that keep to these rules, and one draw needn't show every extreme that they name: Each inv_diag[f] is lower triangular. Tiles of front f with index at least tile_count[f] carry nothing; some front has all 48 tiles live. `tile_owner`: among the 6 tiles of one device (aligned blocks of tiles), no front index is named more than 2 times.
All inputs are finite; a program needn't handle non-finite values.
Results may differ from the reference program's by a relative error of at most 0.0037.
Values may be sent and summed in bfloat16 or wider, within the bound.
No kernel may reach another device: no remote copies, remote signals or barrier semaphores. Data moves between devices by JAX's collectives and lax.ppermute only.
A program may use at most 128 MiB of HBM per device.

```python
import math
import jax
import jax.numpy as jnp
import numpy as np
from jax import lax

PIVOTS = 8192
RHS_COLS = 256
TILE_ROWS = 128
CAPACITY = 2
PARENT_DEV = 512
FRONTS = 4
TILES_DEV = 6
BELOW = 6144
TILES = 48
PARENT = 4096


def draw_inv_diag(key, part):
    first, second = jax.random.split(key)
    lower = jax.random.normal(first, (FRONTS, PIVOTS, PIVOTS), jnp.float32)
    lower = lower * (1.5 / PIVOTS ** 0.5)
    diagonal = jax.random.uniform(second, (FRONTS, PIVOTS), jnp.float32, 0.5, 1.5)
    row_index = lax.broadcasted_iota(jnp.int32, (PIVOTS, PIVOTS), 0)
    col_index = lax.broadcasted_iota(jnp.int32, (PIVOTS, PIVOTS), 1)
    strict = (row_index > col_index)[None]
    on_diag = (row_index == col_index)[None]
    result = jnp.where(strict, lower, 0.0) + jnp.where(on_diag, diagonal[:, :, None], 0.0)
    return result.astype(jnp.bfloat16)


def draw_tile_count(key, part):
    first, second = jax.random.split(key)
    counts = jax.random.randint(first, (FRONTS,), TILES * 3 // 4, TILES + 1, jnp.int32)
    chosen = jax.random.randint(second, (), 0, FRONTS, jnp.int32)
    return jnp.where(jnp.arange(FRONTS, dtype=jnp.int32) == chosen, TILES, counts).astype(jnp.int32)


def with_ends(values, own_key, least, high):
    place = [jax.random.randint(jax.random.fold_in(own_key, axis), (), 0, length) for axis, length in enumerate(values.shape)]
    main_axis = values.shape.index(max(values.shape))
    next_to = place[:main_axis] + [(place[main_axis] + 1) % values.shape[main_axis]] + place[main_axis + 1:]
    return values.at[tuple(place)].set(least).at[tuple(next_to)].set(high)


def levels(key, shape, cuts, least, largest):
    def one(position, blocks):
        draws = jax.random.uniform(jax.random.fold_in(jax.random.fold_in(key, 6), position), (blocks,), jnp.float32, least / len(cuts), largest / len(cuts))
        return jnp.repeat(jnp.exp(draws), shape[position] // blocks).reshape((-1,) + (1,) * (len(shape) - position - 1))

    factor_of = one(*cuts[0])
    for cut in cuts[1:]:
        factor_of = factor_of * one(*cut)
    return factor_of


def routed_block(own_key, own, number, rows, amount, top, limit, skew):
    sequence = jax.random.permutation(own_key, amount)
    crowded, usual = shares(amount, rows * top, limit, skew, True), shares(amount, rows * top, limit, skew, False)
    places = jnp.arange(amount)

    def named(sizes, offset_by):
        used = int((sizes > 0).sum())
        fixed = max(1, used // 4)
        passed = fixed + (places - fixed + offset_by * (used - fixed)) % max(1, amount - fixed)
        return jnp.zeros((amount,), jnp.int32).at[sequence[jnp.where(places < fixed, places, passed)]].set(jnp.asarray(sizes, jnp.int32))

    sizes = jnp.where(number % 4 == 0, named(crowded, number // 4), named(usual, number - number // 4 - 1))
    mixed = jax.random.permutation(jax.random.fold_in(own, 3), amount)
    giver, receiver = mixed[0:amount // 2 * 2:2], mixed[1:amount // 2 * 2:2]
    margin = jnp.minimum(sizes[giver] - 1, limit - sizes[receiver]) // 2
    margin = jnp.where((giver == sequence[0]) | (receiver == sequence[0]) | (sizes[receiver] == 0), 0, jnp.maximum(margin, 0))
    passed = jax.random.randint(jax.random.fold_in(own, 4), (amount // 2,), 0, 1 << 20) % (margin + 1)
    sizes = sizes.at[giver].add(-passed).at[receiver].add(passed)
    items = jnp.searchsorted(jnp.cumsum(sizes), jnp.arange(rows * top), side="right").astype(jnp.int32)
    table = items.reshape(top, rows).T
    table = table[jax.random.permutation(jax.random.fold_in(own, 1), rows)]
    offset_by = jax.random.randint(jax.random.fold_in(own, 2), (rows, 1), 0, top)
    return jnp.take_along_axis(table, (jnp.arange(top)[None, :] + offset_by) % top, axis=1)


def shares(amount, total, bound, slope, full):
    loads = [(1 << 20) // math.isqrt(grade ** slope) + 1 for grade in range(1, amount + 1)]
    largest = bound if full else min(bound, max(-(-total // amount), total * loads[0] // sum(loads)))
    least = 1 if total - largest >= amount - 1 else 0
    given, surplus = [largest] + [least] * (amount - 1), total - largest - least * (amount - 1)
    while surplus > 0:
        free = [i for i in range(1, amount) if given[i] < largest] or [i for i in range(1, amount) if given[i] < bound]
        whole, budget = sum([loads[i] for i in free]), surplus
        for i in free:
            extra = min(bound - given[i], max(1, budget * loads[i] // whole), surplus)
            given[i] = given[i] + extra
            surplus = surplus - extra
    return np.array(given)


def noise(key, extent, spread, most, cuts=(), held_as=jnp.bfloat16):
    gain = levels(key, extent, cuts, -0.22, 0.18) if cuts else 1.0
    values = jax.random.normal(key, extent, jnp.float32) * spread * gain
    return jnp.minimum(jnp.maximum(values, -most), most).astype(held_as)


def setup_inputs(seed: int = 0) -> dict:
    streams_of = jax.random.split(jax.random.key(seed), 8)
    inv_diag = draw_inv_diag(jax.random.fold_in(streams_of[7], 71), 0)
    below = noise(streams_of[1], (FRONTS, BELOW, PIVOTS), PIVOTS ** -0.5, 0.0625, ((0, 4), (1, 8)))
    rhs = noise(streams_of[2], (FRONTS, PIVOTS, RHS_COLS), 1.0, 6.0, ((0, 4), (1, 8)))
    tile_count = draw_tile_count(jax.random.fold_in(streams_of[7], 71), 0)
    tile_owner_keys = jax.random.split(jax.random.fold_in(streams_of[4], 1), FRONTS * TILES // TILES_DEV)
    tile_owner_turns = jax.random.permutation(jax.random.fold_in(streams_of[4], 3), FRONTS * TILES // TILES_DEV)
    tile_owner = jax.vmap(lambda own, number: routed_block(jax.random.fold_in(streams_of[4], 2), own, number, TILES_DEV, FRONTS, 1, CAPACITY, 2))(tile_owner_keys, tile_owner_turns).reshape((FRONTS, TILES, 1))
    tile_rows = with_ends(jax.random.randint(streams_of[5], (FRONTS, TILES, TILE_ROWS), 0, PARENT_DEV), jax.random.fold_in(streams_of[5], 1), 0, PARENT_DEV - 1).astype(jnp.int32)
    parent_rhs = noise(streams_of[6], (FRONTS, PARENT, RHS_COLS), 1.0, 6.0, ((0, 4), (1, 8)))
    return {"inv_diag": inv_diag, "below": below, "rhs": rhs, "tile_count": tile_count, "tile_owner": tile_owner, "tile_rows": tile_rows, "parent_rhs": parent_rhs}


def reference(inv_diag, below, rhs, tile_count, tile_owner, tile_rows, parent_rhs):
    def per_front(front_number):
        solved_one = jnp.dot(inv_diag[front_number], rhs[front_number], preferred_element_type=jnp.float32).astype(jnp.bfloat16)
        update_one = jnp.dot(below[front_number], solved_one, preferred_element_type=jnp.float32).astype(jnp.bfloat16)
        return solved_one, update_one

    solved, updates = lax.map(per_front, jnp.arange(FRONTS, dtype=jnp.int32))
    living = jnp.arange(TILES, dtype=jnp.int32)[None, :] < tile_count[:, None]
    update_tiles = updates.reshape(FRONTS, TILES, TILE_ROWS, RHS_COLS)
    update_tiles = jnp.where(living[:, :, None, None], update_tiles, jnp.zeros_like(update_tiles))
    owners = tile_owner[:, :, 0]
    wide_slot = (jnp.arange(TILES, dtype=jnp.int32) // TILES_DEV)[None, :]
    flat_index = (owners * PARENT + wide_slot * PARENT_DEV)[:, :, None] + tile_rows
    parent_sum = parent_rhs.astype(jnp.float32).reshape(FRONTS * PARENT, RHS_COLS)
    parent_sum = parent_sum.at[flat_index.reshape(-1).astype(jnp.int32)].add(-update_tiles.astype(jnp.float32).reshape(-1, RHS_COLS))
    return solved, parent_sum.reshape(FRONTS, PARENT, RHS_COLS)
```

```python
import jax
import jax.numpy as jnp
from jax import lax
from jax.sharding import PartitionSpec as P

CAPACITY = 2


def ring_order(count):
    if count % 8:
        return list(range(count))
    depth = 4
    columns = count // depth
    walk = [z * columns for z in range(depth)]
    for step, z in enumerate(range(depth - 1, -1, -1)):
        ys = range(1, columns) if step % 2 == 0 else range(columns - 1, 0, -1)
        walk += [z * columns + y for y in ys]
    return walk


def lookup(table, index):
    result = jnp.int32(table[0])
    for place in range(1, len(table)):
        result = jnp.where(index == place, jnp.int32(table[place]), result)
    return result


def dot(a, b):
    return jnp.dot(a, b, preferred_element_type=jnp.float32)


def ring_product(matrix, block, order, place):
    count = len(order)
    rows = block.shape[0]
    half = rows // 2
    onward = [(order[i], order[(i + 1) % count]) for i in range(count)]
    backward = [(b, a) for a, b in onward]

    def part(index, offset, values):
        columns = lax.dynamic_slice_in_dim(matrix, index * rows + offset, values.shape[0], 1)
        return dot(columns, values)

    first, second = block[:half], block[half:]
    total = part(lookup(order, place), 0, block)
    for step in range(1, count):
        first = lax.ppermute(first, "wide", onward)
        second = lax.ppermute(second, "wide", backward)
        from_left = lookup(order, (place + count - step) % count)
        from_right = lookup(order, (place + step) % count)
        total = total + part(from_left, 0, first)
        total = total + part(from_right, half, second)
    return total


def body(inv_diag, below, rhs, tile_count, tile_owner, tile_rows, parent_rhs):
    width = rhs.shape[2]
    tiles = tile_owner.shape[1]
    height = tile_rows.shape[2]
    parent_height = parent_rhs.shape[1]
    fronts = lax.axis_size("front")
    wide = lax.axis_size("wide")
    me = lax.axis_index("front")
    wide_index = lax.axis_index("wide")
    order = ring_order(wide)
    place = lookup([order.index(i) for i in range(wide)], wide_index)

    serial = jnp.arange(tiles, dtype=jnp.int32)
    live_count = jnp.sum(jnp.where(jnp.arange(fronts) == me, tile_count, 0))
    alive = wide_index * tiles + serial < live_count
    owners = tile_owner[0, :, 0]
    same_owner = owners[:, None] == owners[None, :]
    earlier = serial[None, :] < serial[:, None]
    slot = jnp.sum((same_owner & earlier).astype(jnp.int32), axis=1)
    targets = jnp.where(alive[:, None], tile_rows[0], parent_height)

    def chooser_for(owner):
        return (owners[None, :] == owner) & (slot[None, :] == jnp.arange(CAPACITY)[:, None])

    choosers = [chooser_for(me ^ delta) for delta in range(fronts)]
    rows_out = [
        jnp.where(
            jnp.any(c, axis=1)[:, None],
            jnp.sum(jnp.where(c[:, :, None], targets[None], 0), axis=1),
            parent_height,
        )
        for c in choosers
    ]
    swaps = [[(i, i ^ delta) for i in range(fronts)] for delta in range(fronts)]
    rows_in = [rows_out[0]] + [
        lax.ppermute(rows_out[delta], "front", swaps[delta]) for delta in range(1, fronts)
    ]

    solved = ring_product(inv_diag[0], rhs[0], order, place).astype(jnp.bfloat16)
    update = ring_product(below[0], solved, order, place).astype(jnp.bfloat16)
    update = update.reshape(tiles, height, width)
    update = jnp.where(alive[:, None, None], update, jnp.zeros_like(update))
    flat = update.reshape(tiles, height * width)
    values_out = [
        dot(c.astype(jnp.bfloat16), flat).astype(jnp.bfloat16).reshape(CAPACITY * height, width)
        for c in choosers
    ]
    values_in = [values_out[0]] + [
        lax.ppermute(values_out[delta], "front", swaps[delta]) for delta in range(1, fronts)
    ]
    parent_new = parent_rhs[0].astype(jnp.float32)
    numbers = jnp.arange(parent_height, dtype=jnp.int32)[:, None]
    for rows, values in zip(rows_in, values_in):
        hits = (numbers == rows.reshape(1, -1)).astype(jnp.bfloat16)
        parent_new = parent_new - dot(hits, values)
    return (solved[None], parent_new[None])


def solution(mesh):
    split = P("front", "wide", None)
    return jax.shard_map(
        body,
        mesh=mesh,
        in_specs=(split, split, split, P(), split, split, split),
        out_specs=(split, split),
        check_vma=False,
    )
```

```python
import jax
import jax.numpy as jnp
from jax import lax
from jax.sharding import PartitionSpec as P

CAPACITY = 2
LANES = 128
ROUTING_STEP = 2


def ring_order(count):
    if count % 8:
        return list(range(count))
    depth = 4
    columns = count // depth
    walk = [z * columns for z in range(depth)]
    for step, z in enumerate(range(depth - 1, -1, -1)):
        ys = range(1, columns) if step % 2 == 0 else range(columns - 1, 0, -1)
        walk += [z * columns + y for y in ys]
    return walk


def lookup(table, index):
    result = jnp.int32(table[0])
    for place in range(1, len(table)):
        result = jnp.where(index == place, jnp.int32(table[place]), result)
    return result


def dot(a, b):
    return jnp.dot(a, b, preferred_element_type=jnp.float32)


def body(inv_diag, below, rhs, tile_count, tile_owner, tile_rows, parent_rhs):
    width = rhs.shape[2]
    rows = rhs.shape[1]
    half = rows // 2
    tiles = tile_owner.shape[1]
    height = tile_rows.shape[2]
    parent_height = parent_rhs.shape[1]
    fronts = lax.axis_size("front")
    wide = lax.axis_size("wide")
    me = lax.axis_index("front")
    wide_index = lax.axis_index("wide")
    order = ring_order(wide)
    place = lookup([order.index(i) for i in range(wide)], wide_index)
    onward = [(order[i], order[(i + 1) % wide]) for i in range(wide)]
    backward = [(b, a) for a, b in onward]
    from_left = [lookup(order, (place + wide - step) % wide) for step in range(wide)]
    from_right = [lookup(order, (place + step) % wide) for step in range(wide)]

    def part(matrix, index, offset, values):
        columns = lax.dynamic_slice_in_dim(matrix, index * rows + offset, values.shape[0], 1)
        return dot(columns, values)

    def ring_products(matrix, blocks):
        travelling = [(block[:half], block[half:]) for block in blocks]
        totals = [part(matrix, wide_index, 0, block) for block in blocks]
        early = None
        for step in range(1, wide):
            for column, (first, second) in enumerate(travelling):
                first = lax.ppermute(first, "wide", onward)
                second = lax.ppermute(second, "wide", backward)
                travelling[column] = (first, second)
                totals[column] = totals[column] + part(matrix, from_left[step], 0, first)
                totals[column] = totals[column] + part(matrix, from_right[step], half, second)
                if step == ROUTING_STEP:
                    early = first
        return [total.astype(jnp.bfloat16) for total in totals], early

    cuts = range(0, width, LANES)
    solved, early = ring_products(inv_diag[0], [rhs[0][:, c:c + LANES] for c in cuts])

    tile_count, tile_owner, tile_rows, early = lax.optimization_barrier(
        (tile_count, tile_owner, tile_rows, early)
    )
    serial = jnp.arange(tiles, dtype=jnp.int32)
    live_count = jnp.sum(jnp.where(jnp.arange(fronts) == me, tile_count, 0))
    alive = wide_index * tiles + serial < live_count
    owners = tile_owner[0, :, 0]
    same_owner = owners[:, None] == owners[None, :]
    earlier = serial[None, :] < serial[:, None]
    slot = jnp.sum((same_owner & earlier).astype(jnp.int32), axis=1)
    seat = (owners ^ me) * CAPACITY + slot
    slots = fronts * CAPACITY
    chosen = jnp.arange(slots, dtype=jnp.int32)[:, None] == seat[None, :]
    shifted = jnp.where(alive[:, None], tile_rows[0] - parent_height, 0)
    rows_out = parent_height + jnp.sum(jnp.where(chosen[:, :, None], shifted[None], 0), axis=1)
    rows_out = rows_out.reshape(fronts, CAPACITY * height)
    swaps = [[(i, i ^ delta) for i in range(fronts)] for delta in range(fronts)]
    rows_in = [rows_out[0]] + [
        lax.ppermute(rows_out[delta], "front", swaps[delta]) for delta in range(1, fronts)
    ]
    picker = (
        jnp.arange(slots * height, dtype=jnp.int32)[:, None]
        == (seat[:, None] * height + jnp.arange(height, dtype=jnp.int32)[None, :]).reshape(1, -1)
    ).astype(jnp.bfloat16)
    picker = picker.reshape(fronts, CAPACITY * height, tiles * height)
    alive_rows = jnp.broadcast_to(alive[:, None], (tiles, height)).reshape(-1, 1)
    numbers = jnp.arange(parent_height, dtype=jnp.int32)[:, None]

    updates, _ = ring_products(below[0], solved)
    results = []
    for c, update in zip(cuts, updates):
        update = jnp.where(alive_rows, update, jnp.zeros_like(update))
        values_out = [dot(picker[delta], update).astype(jnp.bfloat16) for delta in range(fronts)]
        values_in = [values_out[0]] + [
            lax.ppermute(values_out[delta], "front", swaps[delta]) for delta in range(1, fronts)
        ]
        total = parent_rhs[0][:, c:c + LANES].astype(jnp.float32)
        for rows_here, values in zip(rows_in, values_in):
            hits = (numbers == rows_here[None, :]).astype(jnp.bfloat16)
            total = total - dot(hits, values)
        results.append(total)
    return (
        jnp.concatenate(solved, axis=1)[None],
        jnp.concatenate(results, axis=1)[None],
    )


def solution(mesh):
    split = P("front", "wide", None)
    return jax.shard_map(
        body,
        mesh=mesh,
        in_specs=(split, split, split, P(), split, split, split),
        out_specs=(split, split),
        check_vma=False,
    )
```

```python
import jax
import jax.numpy as jnp
from jax import lax
from jax.sharding import PartitionSpec as P

CAPACITY = 2
LANES = 128
ROUTING_STEPS = (2, 4)


def ring_order(count):
    if count % 8:
        return list(range(count))
    depth = 4
    columns = count // depth
    walk = [z * columns for z in range(depth)]
    for step, z in enumerate(range(depth - 1, -1, -1)):
        ys = range(1, columns) if step % 2 == 0 else range(columns - 1, 0, -1)
        walk += [z * columns + y for y in ys]
    return walk


def lookup(table, index):
    result = jnp.int32(table[0])
    for place in range(1, len(table)):
        result = jnp.where(index == place, jnp.int32(table[place]), result)
    return result


def dot(a, b):
    return jnp.dot(a, b, preferred_element_type=jnp.float32)


def body(inv_diag, below, rhs, tile_count, tile_owner, tile_rows, parent_rhs):
    width = rhs.shape[2]
    rows = rhs.shape[1]
    half = rows // 2
    tiles = tile_owner.shape[1]
    height = tile_rows.shape[2]
    parent_height = parent_rhs.shape[1]
    fronts = lax.axis_size("front")
    wide = lax.axis_size("wide")
    me = lax.axis_index("front")
    wide_index = lax.axis_index("wide")
    order = ring_order(wide)
    place = lookup([order.index(i) for i in range(wide)], wide_index)
    onward = [(order[i], order[(i + 1) % wide]) for i in range(wide)]
    backward = [(b, a) for a, b in onward]
    from_left = [lookup(order, (place + wide - step) % wide) for step in range(wide)]
    from_right = [lookup(order, (place + step) % wide) for step in range(wide)]

    def part(matrix, index, offset, values):
        columns = lax.dynamic_slice_in_dim(matrix, index * rows + offset, values.shape[0], 1)
        return dot(columns, values)

    def ring_products(matrix, blocks, aside=None):
        travelling = [(block[:half], block[half:]) for block in blocks]
        totals = [part(matrix, wide_index, 0, block) for block in blocks]
        extra = None
        for step in range(1, wide):
            for column, (first, second) in enumerate(travelling):
                first = lax.ppermute(first, "wide", onward)
                second = lax.ppermute(second, "wide", backward)
                if aside and column == 0 and step == ROUTING_STEPS[0]:
                    extra, first = aside(first)
                if aside and column == 0 and step == ROUTING_STEPS[1]:
                    first, extra = lax.optimization_barrier((first, extra))
                travelling[column] = (first, second)
                totals[column] = totals[column] + part(matrix, from_left[step], 0, first)
                totals[column] = totals[column] + part(matrix, from_right[step], half, second)
        return [total.astype(jnp.bfloat16) for total in totals], extra

    swaps = [[(i, i ^ delta) for i in range(fronts)] for delta in range(fronts)]

    def routing(after):
        counts, owners, places, after = lax.optimization_barrier(
            (tile_count, tile_owner, tile_rows, after)
        )
        serial = jnp.arange(tiles, dtype=jnp.int32)
        live_count = jnp.sum(jnp.where(jnp.arange(fronts) == me, counts, 0))
        alive = wide_index * tiles + serial < live_count
        owners = owners[0, :, 0]
        same_owner = owners[:, None] == owners[None, :]
        earlier = serial[None, :] < serial[:, None]
        slot = jnp.sum((same_owner & earlier).astype(jnp.int32), axis=1)
        seat = (owners ^ me) * CAPACITY + slot
        slots = fronts * CAPACITY
        chosen = jnp.arange(slots, dtype=jnp.int32)[:, None] == seat[None, :]
        shifted = jnp.where(alive[:, None], places[0] - parent_height, 0)
        rows_out = parent_height + jnp.sum(jnp.where(chosen[:, :, None], shifted[None], 0), axis=1)
        rows_out = rows_out.reshape(fronts, CAPACITY * height)
        rows_in = [rows_out[0]] + [
            lax.ppermute(rows_out[delta], "front", swaps[delta]) for delta in range(1, fronts)
        ]
        picker = (
            jnp.arange(slots * height, dtype=jnp.int32)[:, None]
            == (seat[:, None] * height + jnp.arange(height, dtype=jnp.int32)[None, :]).reshape(1, -1)
        ).astype(jnp.bfloat16)
        picker = picker.reshape(fronts, CAPACITY * height, tiles * height)
        alive_rows = jnp.broadcast_to(alive[:, None], (tiles, height)).reshape(-1, 1)
        return (rows_in, picker, alive_rows), after

    cuts = range(0, width, LANES)
    solved, (rows_in, picker, alive_rows) = ring_products(
        inv_diag[0], [rhs[0][:, c:c + LANES] for c in cuts], routing
    )
    numbers = jnp.arange(parent_height, dtype=jnp.int32)[:, None]

    updates, _ = ring_products(below[0], solved)
    results = []
    for c, update in zip(cuts, updates):
        update = jnp.where(alive_rows, update, jnp.zeros_like(update))
        values_out = [dot(picker[delta], update).astype(jnp.bfloat16) for delta in range(fronts)]
        values_in = [values_out[0]] + [
            lax.ppermute(values_out[delta], "front", swaps[delta]) for delta in range(1, fronts)
        ]
        total = parent_rhs[0][:, c:c + LANES].astype(jnp.float32)
        for rows_here, values in zip(rows_in, values_in):
            hits = (numbers == rows_here[None, :]).astype(jnp.bfloat16)
            total = total - dot(hits, values)
        results.append(total)
    return (
        jnp.concatenate(solved, axis=1)[None],
        jnp.concatenate(results, axis=1)[None],
    )


def solution(mesh):
    split = P("front", "wide", None)
    return jax.shard_map(
        body,
        mesh=mesh,
        in_specs=(split, split, split, P(), split, split, split),
        out_specs=(split, split),
        check_vma=False,
    )
```

```python
import jax
import jax.numpy as jnp
from jax import lax
from jax.experimental import pallas as pl
from jax.experimental.layout import Layout, with_layout_constraint
from jax.experimental.pallas import tpu as pltpu
from jax.sharding import PartitionSpec as P

CAPACITY = 2
LANES = 128
ROUTING_STEPS = (2, 4)


def ring_order(count):
    if count % 8:
        return list(range(count))
    depth = 4
    columns = count // depth
    walk = [z * columns for z in range(depth)]
    for step, z in enumerate(range(depth - 1, -1, -1)):
        ys = range(1, columns) if step % 2 == 0 else range(columns - 1, 0, -1)
        walk += [z * columns + y for y in ys]
    return walk


def lookup(table, index):
    result = jnp.int32(table[0])
    for place in range(1, len(table)):
        result = jnp.where(index == place, jnp.int32(table[place]), result)
    return result


def row_major(array):
    return with_layout_constraint(array, Layout(major_to_minor=tuple(range(array.ndim))))


def dot(a, b):
    return row_major(jnp.dot(a, b, preferred_element_type=jnp.float32))


def held(matrix):
    def kernel(source, target, semaphore):
        copy = pltpu.make_async_copy(source, target, semaphore)
        copy.start()
        copy.wait()

    return pl.pallas_call(
        kernel,
        out_shape=pltpu.VMEM(matrix.shape, matrix.dtype),
        in_specs=[pl.BlockSpec(memory_space=pl.ANY)],
        out_specs=pl.BlockSpec(memory_space=pltpu.VMEM),
        scratch_shapes=[pltpu.SemaphoreType.DMA],
        compiler_params=pltpu.CompilerParams(vmem_limit_bytes=2 << 20),
        cost_estimate=pl.CostEstimate(
            flops=0, bytes_accessed=2 * matrix.size * matrix.dtype.itemsize, transcendentals=0
        ),
    )(matrix)


def body(inv_diag, below, rhs, tile_count, tile_owner, tile_rows, parent_rhs):
    width = rhs.shape[2]
    rows = rhs.shape[1]
    half = rows // 2
    tiles = tile_owner.shape[1]
    height = tile_rows.shape[2]
    parent_height = parent_rhs.shape[1]
    fronts = lax.axis_size("front")
    wide = lax.axis_size("wide")
    me = lax.axis_index("front")
    wide_index = lax.axis_index("wide")
    order = ring_order(wide)
    place = lookup([order.index(i) for i in range(wide)], wide_index)
    onward = [(order[i], order[(i + 1) % wide]) for i in range(wide)]
    backward = [(b, a) for a, b in onward]
    from_left = [lookup(order, (place + wide - step) % wide) for step in range(wide)]
    from_right = [lookup(order, (place + step) % wide) for step in range(wide)]

    def part(matrix, index, offset, values):
        columns = lax.dynamic_slice_in_dim(matrix, index * rows + offset, values.shape[0], 1)
        return dot(columns, values)

    def ring_products(matrix, blocks, aside=None):
        travelling = [(block[:half], block[half:]) for block in blocks]
        total = part(matrix, wide_index, 0, jnp.concatenate(blocks, axis=1))
        extra = None
        for step in range(1, wide):
            for column, (first, second) in enumerate(travelling):
                first = lax.ppermute(first, "wide", onward)
                second = lax.ppermute(second, "wide", backward)
                if aside and column == 0 and step == ROUTING_STEPS[0]:
                    extra, first = aside(first)
                if aside and column == 0 and step == ROUTING_STEPS[1]:
                    first, extra = lax.optimization_barrier((first, extra))
                travelling[column] = (first, second)
            if step < wide - 1:
                firsts, seconds = [jnp.concatenate(pieces, axis=1) for pieces in zip(*travelling)]
                total = total + part(matrix, from_left[step], 0, firsts)
                total = total + part(matrix, from_right[step], half, seconds)
        results = []
        for column, (first, second) in enumerate(travelling):
            piece = total[:, column * LANES:(column + 1) * LANES]
            piece = piece + part(matrix, from_left[wide - 1], 0, first)
            piece = piece + part(matrix, from_right[wide - 1], half, second)
            results.append(piece.astype(jnp.bfloat16))
        return results, extra

    swaps = [[(i, i ^ delta) for i in range(fronts)] for delta in range(fronts)]

    def routing(after):
        counts, owners, places, after = lax.optimization_barrier(
            (tile_count, tile_owner, tile_rows, after)
        )
        serial = jnp.arange(tiles, dtype=jnp.int32)
        live_count = jnp.sum(jnp.where(jnp.arange(fronts) == me, counts, 0))
        alive = wide_index * tiles + serial < live_count
        owners = owners[0, :, 0]
        same_owner = owners[:, None] == owners[None, :]
        earlier = serial[None, :] < serial[:, None]
        slot = jnp.sum((same_owner & earlier).astype(jnp.int32), axis=1)
        seat = (owners ^ me) * CAPACITY + slot
        slots = fronts * CAPACITY
        chosen = jnp.arange(slots, dtype=jnp.int32)[:, None] == seat[None, :]
        shifted = jnp.where(alive[:, None], places[0] - parent_height, 0)
        rows_out = parent_height + jnp.sum(jnp.where(chosen[:, :, None], shifted[None], 0), axis=1)
        rows_out = rows_out.reshape(fronts, CAPACITY * height)
        rows_in = [rows_out[0]] + [
            lax.ppermute(rows_out[delta], "front", swaps[delta]) for delta in range(1, fronts)
        ]
        picker = (
            jnp.arange(slots * height, dtype=jnp.int32)[:, None]
            == (seat[:, None] * height + jnp.arange(height, dtype=jnp.int32)[None, :]).reshape(1, -1)
        ).astype(jnp.bfloat16)
        picker = picker.reshape(fronts, CAPACITY * height, tiles * height)
        alive_rows = jnp.broadcast_to(alive[:, None], (tiles, height)).reshape(-1, 1)
        return (rows_in, picker, alive_rows), after

    cuts = range(0, width, LANES)
    solved, (rows_in, picker, alive_rows) = ring_products(
        held(inv_diag[0]), [rhs[0][:, c:c + LANES] for c in cuts], routing
    )
    numbers = jnp.arange(parent_height, dtype=jnp.int32)[:, None]

    updates, _ = ring_products(held(below[0]), solved)
    results = []
    for c, update in zip(cuts, updates):
        update = jnp.where(alive_rows, update, jnp.zeros_like(update))
        values_out = [dot(picker[delta], update).astype(jnp.bfloat16) for delta in range(fronts)]
        values_in = [values_out[0]] + [
            lax.ppermute(values_out[delta], "front", swaps[delta]) for delta in range(1, fronts)
        ]
        total = parent_rhs[0][:, c:c + LANES].astype(jnp.float32)
        for rows_here, values in zip(rows_in, values_in):
            hits = (numbers == rows_here[None, :]).astype(jnp.bfloat16)
            total = total - dot(hits, values)
        results.append(total)
    return (
        jnp.concatenate(solved, axis=1)[None],
        jnp.concatenate(results, axis=1)[None],
    )


def solution(mesh):
    split = P("front", "wide", None)
    return jax.shard_map(
        body,
        mesh=mesh,
        in_specs=(split, split, split, P(), split, split, split),
        out_specs=(split, split),
        check_vma=False,
    )
```

```python
import jax
import jax.numpy as jnp
from jax import lax
from jax.experimental import pallas as pl
from jax.experimental.layout import Layout, with_layout_constraint
from jax.experimental.pallas import tpu as pltpu
from jax.sharding import PartitionSpec as P

CAPACITY = 2
LANES = 128
ROUTING_STEPS = (2, 4)


def ring_order(count):
    if count % 8:
        return list(range(count))
    depth = 4
    columns = count // depth
    walk = [z * columns for z in range(depth)]
    for step, z in enumerate(range(depth - 1, -1, -1)):
        ys = range(1, columns) if step % 2 == 0 else range(columns - 1, 0, -1)
        walk += [z * columns + y for y in ys]
    return walk


def lookup(table, index):
    result = jnp.int32(table[0])
    for place in range(1, len(table)):
        result = jnp.where(index == place, jnp.int32(table[place]), result)
    return result


def row_major(array):
    return with_layout_constraint(array, Layout(major_to_minor=tuple(range(array.ndim))))


def dot(a, b):
    return row_major(jnp.dot(a, b, preferred_element_type=jnp.float32))


def streamed_product(matrix, total, firsts, seconds, order, step):
    count = len(order)
    height = matrix.shape[0]
    half = firsts[0].shape[0]
    pieces = len(firsts)
    chunk = 256 if height % 256 == 0 else height
    chunks = height // chunk
    given = 0 if total is None else 1

    def kernel(source, *refs):
        first_refs = refs[given:given + pieces]
        second_refs = refs[given + pieces:given + 2 * pieces]
        out, buffers, semaphores = refs[given + 2 * pieces:]
        place = lookup([order.index(i) for i in range(count)], lax.axis_index("wide"))
        columns = [
            2 * half * lookup(order, lax.rem(place + count - step, count)),
            2 * half * lookup(order, lax.rem(place + step, count)) + half,
        ]
        copies = []
        for number in range(chunks):
            part = pl.ds(number * chunk, chunk)
            for side in range(2):
                start = pl.multiple_of(columns[side], half)
                copies.append(
                    pltpu.make_async_copy(
                        source.at[part, pl.ds(start, half)],
                        buffers.at[side, part],
                        semaphores.at[side, number],
                    )
                )
                copies[-1].start()
        values = [
            jnp.concatenate([ref[...] for ref in refs_], axis=1)
            for refs_ in (first_refs, second_refs)
        ]
        for number in range(chunks):
            part = pl.ds(number * chunk, chunk)
            result = refs[0][part, :] if given else 0.0
            for side in range(2):
                copies[2 * number + side].wait()
                result = result + jnp.dot(
                    buffers[side, part], values[side], preferred_element_type=jnp.float32
                )
            out[part, :] = result

    width = sum(piece.shape[1] for piece in firsts)
    blocks = [pl.BlockSpec(memory_space=pltpu.VMEM)] * (given + 2 * pieces)
    inputs = ([total] if given else []) + list(firsts) + list(seconds)
    return pl.pallas_call(
        kernel,
        out_shape=pltpu.VMEM((height, width), jnp.float32),
        in_specs=[pl.BlockSpec(memory_space=pltpu.HBM)] + blocks,
        out_specs=pl.BlockSpec(memory_space=pltpu.VMEM),
        scratch_shapes=[
            pltpu.VMEM((2, height, half), matrix.dtype),
            pltpu.SemaphoreType.DMA((2, chunks)),
        ],
        input_output_aliases={1: 0} if given else {},
        compiler_params=pltpu.CompilerParams(vmem_limit_bytes=16 << 20),
        cost_estimate=pl.CostEstimate(
            flops=4 * height * half * width,
            bytes_accessed=4 * height * half + 8 * height * width,
            transcendentals=0,
        ),
    )(pltpu.with_memory_space_constraint(matrix, pltpu.HBM), *inputs)


def body(inv_diag, below, rhs, tile_count, tile_owner, tile_rows, parent_rhs):
    width = rhs.shape[2]
    rows = rhs.shape[1]
    half = rows // 2
    tiles = tile_owner.shape[1]
    height = tile_rows.shape[2]
    parent_height = parent_rhs.shape[1]
    fronts = lax.axis_size("front")
    wide = lax.axis_size("wide")
    me = lax.axis_index("front")
    wide_index = lax.axis_index("wide")
    order = ring_order(wide)
    place = lookup([order.index(i) for i in range(wide)], wide_index)
    onward = [(order[i], order[(i + 1) % wide]) for i in range(wide)]
    backward = [(b, a) for a, b in onward]
    def ring_products(matrix, blocks, aside=None):
        travelling = [(block[:half], block[half:]) for block in blocks]
        total = None
        extra = None
        for step in range(1, wide):
            arrived = list(travelling)
            if step > 1:
                first, second = travelling[0]
                first, total = lax.optimization_barrier((first, total))
                travelling[0] = (first, second)
            for column, (first, second) in enumerate(travelling):
                first = lax.ppermute(first, "wide", onward)
                second = lax.ppermute(second, "wide", backward)
                if aside and column == 0 and step == ROUTING_STEPS[0]:
                    extra, first = aside(first)
                if aside and column == 0 and step == ROUTING_STEPS[1]:
                    first, extra = lax.optimization_barrier((first, extra))
                travelling[column] = (first, second)
            firsts, seconds = zip(*arrived)
            total = streamed_product(matrix, total, firsts, seconds, order, step - 1)
        results = []
        for column, (first, second) in enumerate(travelling):
            piece = total[:, column * LANES:(column + 1) * LANES]
            piece = streamed_product(matrix, piece, [first], [second], order, wide - 1)
            results.append(piece.astype(jnp.bfloat16))
        return results, extra

    swaps = [[(i, i ^ delta) for i in range(fronts)] for delta in range(fronts)]

    def routing(after):
        counts, owners, places, after = lax.optimization_barrier(
            (tile_count, tile_owner, tile_rows, after)
        )
        serial = jnp.arange(tiles, dtype=jnp.int32)
        live_count = jnp.sum(jnp.where(jnp.arange(fronts) == me, counts, 0))
        alive = wide_index * tiles + serial < live_count
        owners = owners[0, :, 0]
        same_owner = owners[:, None] == owners[None, :]
        earlier = serial[None, :] < serial[:, None]
        slot = jnp.sum((same_owner & earlier).astype(jnp.int32), axis=1)
        seat = (owners ^ me) * CAPACITY + slot
        slots = fronts * CAPACITY
        chosen = jnp.arange(slots, dtype=jnp.int32)[:, None] == seat[None, :]
        shifted = jnp.where(alive[:, None], places[0] - parent_height, 0)
        rows_out = parent_height + jnp.sum(jnp.where(chosen[:, :, None], shifted[None], 0), axis=1)
        rows_out = rows_out.reshape(fronts, CAPACITY * height)
        rows_in = [rows_out[0]] + [
            lax.ppermute(rows_out[delta], "front", swaps[delta]) for delta in range(1, fronts)
        ]
        picker = (
            jnp.arange(slots * height, dtype=jnp.int32)[:, None]
            == (seat[:, None] * height + jnp.arange(height, dtype=jnp.int32)[None, :]).reshape(1, -1)
        ).astype(jnp.bfloat16)
        picker = picker.reshape(fronts, CAPACITY * height, tiles * height)
        alive_rows = jnp.broadcast_to(alive[:, None], (tiles, height)).reshape(-1, 1)
        return (rows_in, picker, alive_rows), after

    cuts = range(0, width, LANES)
    solved, (rows_in, picker, alive_rows) = ring_products(
        inv_diag[0], [rhs[0][:, c:c + LANES] for c in cuts], routing
    )
    numbers = jnp.arange(parent_height, dtype=jnp.int32)[:, None]

    updates, _ = ring_products(below[0], solved)
    results = []
    for c, update in zip(cuts, updates):
        update = jnp.where(alive_rows, update, jnp.zeros_like(update))
        values_out = [dot(picker[delta], update).astype(jnp.bfloat16) for delta in range(fronts)]
        values_in = [values_out[0]] + [
            lax.ppermute(values_out[delta], "front", swaps[delta]) for delta in range(1, fronts)
        ]
        total = parent_rhs[0][:, c:c + LANES].astype(jnp.float32)
        for rows_here, values in zip(rows_in, values_in):
            hits = (numbers == rows_here[None, :]).astype(jnp.bfloat16)
            total = total - dot(hits, values)
        results.append(total)
    return (
        jnp.concatenate(solved, axis=1)[None],
        jnp.concatenate(results, axis=1)[None],
    )


def solution(mesh):
    split = P("front", "wide", None)
    return jax.shard_map(
        body,
        mesh=mesh,
        in_specs=(split, split, split, P(), split, split, split),
        out_specs=(split, split),
        check_vma=False,
    )
```

```python
import jax
import jax.numpy as jnp
from jax import lax
from jax.experimental import pallas as pl
from jax.experimental.layout import Layout, with_layout_constraint
from jax.experimental.pallas import tpu as pltpu
from jax.sharding import PartitionSpec as P

CAPACITY = 2
LANES = 128
DEPTH = 4


def row_major(array):
    return with_layout_constraint(array, Layout(major_to_minor=tuple(range(array.ndim))))


def dot(a, b):
    return row_major(jnp.dot(a, b, preferred_element_type=jnp.float32))


def held(matrix):
    def kernel(source, target, semaphore):
        copy = pltpu.make_async_copy(source, target, semaphore)
        copy.start()
        copy.wait()

    return pl.pallas_call(
        kernel,
        out_shape=pltpu.VMEM(matrix.shape, matrix.dtype),
        in_specs=[pl.BlockSpec(memory_space=pl.ANY)],
        out_specs=pl.BlockSpec(memory_space=pltpu.VMEM),
        scratch_shapes=[pltpu.SemaphoreType.DMA],
        compiler_params=pltpu.CompilerParams(vmem_limit_bytes=2 << 20),
        cost_estimate=pl.CostEstimate(
            flops=0, bytes_accessed=2 * matrix.size * matrix.dtype.itemsize, transcendentals=0
        ),
    )(pltpu.with_memory_space_constraint(matrix, pltpu.HBM))


def body(inv_diag, below, rhs, tile_count, tile_owner, tile_rows, parent_rhs):
    width = rhs.shape[2]
    rows = rhs.shape[1]
    tiles = tile_owner.shape[1]
    height = tile_rows.shape[2]
    parent_height = parent_rhs.shape[1]
    fronts = lax.axis_size("front")
    wide = lax.axis_size("wide")
    me = lax.axis_index("front")
    wide_index = lax.axis_index("wide")
    depth = DEPTH if wide % DEPTH == 0 else 1
    across = wide // depth
    z, y = wide_index // across, wide_index % across
    z_ring = [(i, (i + across) % wide) for i in range(wide)]
    y_shifts = [
        [(i, i // across * across + (i + shift) % across) for i in range(wide)]
        for shift in range(across)
    ]

    def block_of(step, shift):
        return (z + depth - step) % depth * across + (y + across - shift) % across

    def part(matrix, step, shift, values):
        columns = lax.dynamic_slice_in_dim(matrix, block_of(step, shift) * rows, rows, 1)
        return dot(columns, values)

    def gathered_product(matrix, blocks, later=None, aside=None):
        column_count = len(blocks)
        held_now = list(blocks)
        total = part(matrix, 0, 0, jnp.concatenate(blocks, axis=1))
        waiting = []
        extra = None
        for step in range(depth):
            if step:
                held_now = following
                held_now[0], total, later = lax.optimization_barrier((held_now[0], total, later))
            if aside and step == 1:
                extra, held_now[0] = aside(held_now[0])
            if aside and step == depth - 1:
                held_now[0], extra = lax.optimization_barrier((held_now[0], extra))
            following = [lax.ppermute(b, "wide", z_ring) for b in held_now] if step < depth - 1 else None
            passed = [
                [lax.ppermute(b, "wide", y_shifts[shift]) for b in held_now]
                for shift in range(1, across)
            ]
            if step:
                total = total + part(matrix, step, 0, jnp.concatenate(held_now, axis=1))
            for at, shift, pieces in waiting:
                total = total + part(matrix, at, shift, jnp.concatenate(pieces, axis=1))
            waiting = [(step, shift, passed[shift - 1]) for shift in range(1, across)]
        results = []
        for column in range(column_count):
            piece = total[:, column * LANES:(column + 1) * LANES]
            for at, shift, pieces in waiting:
                piece = piece + part(matrix, at, shift, pieces[column])
            results.append(piece.astype(jnp.bfloat16))
        return results, later, extra

    swaps = [[(i, i ^ delta) for i in range(fronts)] for delta in range(fronts)]

    def routing(after):
        counts, owners, places, after = lax.optimization_barrier(
            (tile_count, tile_owner, tile_rows, after)
        )
        serial = jnp.arange(tiles, dtype=jnp.int32)
        live_count = jnp.sum(jnp.where(jnp.arange(fronts) == me, counts, 0))
        alive = wide_index * tiles + serial < live_count
        owners = owners[0, :, 0]
        same_owner = owners[:, None] == owners[None, :]
        earlier = serial[None, :] < serial[:, None]
        slot = jnp.sum((same_owner & earlier).astype(jnp.int32), axis=1)
        seat = (owners ^ me) * CAPACITY + slot
        slots = fronts * CAPACITY
        chosen = jnp.arange(slots, dtype=jnp.int32)[:, None] == seat[None, :]
        shifted = jnp.where(alive[:, None], places[0] - parent_height, 0)
        rows_out = parent_height + jnp.sum(jnp.where(chosen[:, :, None], shifted[None], 0), axis=1)
        rows_out = rows_out.reshape(fronts, CAPACITY * height)
        rows_in = [rows_out[0]] + [
            lax.ppermute(rows_out[delta], "front", swaps[delta]) for delta in range(1, fronts)
        ]
        picker = (
            jnp.arange(slots * height, dtype=jnp.int32)[:, None]
            == (seat[:, None] * height + jnp.arange(height, dtype=jnp.int32)[None, :]).reshape(1, -1)
        ).astype(jnp.bfloat16)
        picker = picker.reshape(fronts, CAPACITY * height, tiles * height)
        alive_rows = jnp.broadcast_to(alive[:, None], (tiles, height)).reshape(-1, 1)
        return (rows_in, picker, alive_rows), after

    cuts = range(0, width, LANES)
    solved, below_rows, (rows_in, picker, alive_rows) = gathered_product(
        held(inv_diag[0]), [rhs[0][:, c:c + LANES] for c in cuts], held(below[0]), routing
    )
    numbers = jnp.arange(parent_height, dtype=jnp.int32)[:, None]

    updates, _, _ = gathered_product(below_rows, solved)
    results = []
    for c, update in zip(cuts, updates):
        update = jnp.where(alive_rows, update, jnp.zeros_like(update))
        values_out = [dot(picker[delta], update).astype(jnp.bfloat16) for delta in range(fronts)]
        values_in = [values_out[0]] + [
            lax.ppermute(values_out[delta], "front", swaps[delta]) for delta in range(1, fronts)
        ]
        total = parent_rhs[0][:, c:c + LANES].astype(jnp.float32)
        for rows_here, values in zip(rows_in, values_in):
            hits = (numbers == rows_here[None, :]).astype(jnp.bfloat16)
            total = total - dot(hits, values)
        results.append(total)
    return (
        jnp.concatenate(solved, axis=1)[None],
        jnp.concatenate(results, axis=1)[None],
    )


def solution(mesh):
    split = P("front", "wide", None)
    return jax.shard_map(
        body,
        mesh=mesh,
        in_specs=(split, split, split, P(), split, split, split),
        out_specs=(split, split),
        check_vma=False,
    )
```

```python
import jax
import jax.numpy as jnp
from jax import lax
from jax.experimental.layout import Layout, with_layout_constraint
from jax.sharding import PartitionSpec as P

CAPACITY = 2
DEPTH = 4


def row_major(array):
    return with_layout_constraint(array, Layout(major_to_minor=tuple(range(array.ndim))))


def dot(a, b):
    return row_major(jnp.dot(a, b, preferred_element_type=jnp.float32))


def body(inv_diag, below, rhs, tile_count, tile_owner, tile_rows, parent_rhs):
    rows = rhs.shape[1]
    tiles = tile_owner.shape[1]
    height = tile_rows.shape[2]
    parent_height = parent_rhs.shape[1]
    fronts = lax.axis_size("front")
    wide = lax.axis_size("wide")
    me = lax.axis_index("front")
    wide_index = lax.axis_index("wide")
    depth = DEPTH if wide % DEPTH == 0 else 1
    across = wide // depth
    y = wide_index % across
    z_groups = [[i * across + j for i in range(depth)] for j in range(across)]
    y_shifts = [
        [(i, i // across * across + (i + shift) % across) for i in range(wide)]
        for shift in range(across)
    ]
    quarter = rows // 4
    share = (rows - quarter) // 2

    def along_z(values):
        return lax.all_gather(values, "wide", axis=0, tiled=True, axis_index_groups=z_groups)

    def along_y(values):
        return [lax.ppermute(values, "wide", y_shifts[shift]) for shift in range(1, across)]

    def columns_of(matrix, shifts, offset, length):
        return jnp.concatenate(
            [
                lax.dynamic_slice_in_dim(
                    matrix,
                    (i * across + (y + across - shift) % across) * rows + offset,
                    length,
                    1,
                )
                for i in range(depth)
                for shift in shifts
            ],
            axis=1,
        )

    def assembled(matrix):
        result = []
        for part in range(2):
            for shift in range(across):
                result.append(columns_of(matrix, [shift], part * share, share))
        result.append(columns_of(matrix, range(across), 2 * share, quarter))
        return result

    def gathered_product(matrices, block, later=None, aside=None):
        extra = None
        corner = block[2 * share:]
        corners = [corner] + along_y(corner)
        first_part, second_part = block[:share], block[share:2 * share]
        first = along_z(first_part)
        second_part, corners = lax.optimization_barrier((second_part, corners))
        second = along_z(second_part)
        first, matrices, corners = lax.optimization_barrier((first, matrices, corners))
        third = along_z(jnp.concatenate(corners, axis=0))
        passed = along_y(first)
        if aside:
            extra, passed[0] = aside(passed[0])
            second, later, extra = lax.optimization_barrier((second, later, extra))
        arrived = [first] + passed + [second] + along_y(second) + [third]
        total = None
        for matrix, values in zip(matrices, arrived):
            product = dot(matrix, values)
            total = product if total is None else total + product
        return total.astype(jnp.bfloat16), later, extra

    swaps = [[(i, i ^ delta) for i in range(fronts)] for delta in range(fronts)]

    def routing(after):
        counts, owners, places, after = lax.optimization_barrier(
            (tile_count, tile_owner, tile_rows, after)
        )
        serial = jnp.arange(tiles, dtype=jnp.int32)
        live_count = jnp.sum(jnp.where(jnp.arange(fronts) == me, counts, 0))
        alive = wide_index * tiles + serial < live_count
        owners = owners[0, :, 0]
        same_owner = owners[:, None] == owners[None, :]
        earlier = serial[None, :] < serial[:, None]
        slot = jnp.sum((same_owner & earlier).astype(jnp.int32), axis=1)
        seat = (owners ^ me) * CAPACITY + slot
        slots = fronts * CAPACITY
        chosen = jnp.arange(slots, dtype=jnp.int32)[:, None] == seat[None, :]
        shifted = jnp.where(alive[:, None], places[0] - parent_height, 0)
        rows_out = parent_height + jnp.sum(jnp.where(chosen[:, :, None], shifted[None], 0), axis=1)
        rows_out = rows_out.reshape(fronts, CAPACITY * height)
        rows_in = [rows_out[0]] + [
            lax.ppermute(rows_out[delta], "front", swaps[delta]) for delta in range(1, fronts)
        ]
        picker = (
            jnp.arange(slots * height, dtype=jnp.int32)[:, None]
            == (seat[:, None] * height + jnp.arange(height, dtype=jnp.int32)[None, :]).reshape(1, -1)
        ).astype(jnp.bfloat16)
        picker = picker.reshape(fronts, CAPACITY * height, tiles * height)
        alive_rows = jnp.broadcast_to(alive[:, None], (tiles, height)).reshape(-1, 1)
        return (rows_in, picker, alive_rows), after

    solved, below_parts, (rows_in, picker, alive_rows) = gathered_product(
        assembled(inv_diag[0]), rhs[0], assembled(below[0]), routing
    )
    numbers = jnp.arange(parent_height, dtype=jnp.int32)[:, None]

    update, _, _ = gathered_product(below_parts, solved)
    update = jnp.where(alive_rows, update, jnp.zeros_like(update))
    values_out = [dot(picker[delta], update).astype(jnp.bfloat16) for delta in range(fronts)]
    values_in = [values_out[0]] + [
        lax.ppermute(values_out[delta], "front", swaps[delta]) for delta in range(1, fronts)
    ]
    parent_new = parent_rhs[0].astype(jnp.float32)
    for rows_here, values in zip(rows_in, values_in):
        hits = (numbers == rows_here[None, :]).astype(jnp.bfloat16)
        parent_new = parent_new - dot(hits, values)
    return (solved[None], parent_new[None])


def solution(mesh):
    split = P("front", "wide", None)
    return jax.shard_map(
        body,
        mesh=mesh,
        in_specs=(split, split, split, P(), split, split, split),
        out_specs=(split, split),
        check_vma=False,
    )
```

```python
import jax
import jax.numpy as jnp
from jax import lax
from jax.sharding import PartitionSpec as P

CAPACITY = 2
CHAINS = 2
ROUTING_STEPS = (2, 4)


def ring_order(count):
    if count % 8:
        return list(range(count))
    depth = 4
    columns = count // depth
    walk = [z * columns for z in range(depth)]
    for step, z in enumerate(range(depth - 1, -1, -1)):
        ys = range(1, columns) if step % 2 == 0 else range(columns - 1, 0, -1)
        walk += [z * columns + y for y in ys]
    return walk


def lookup(table, index):
    result = jnp.int32(table[0])
    for place in range(1, len(table)):
        result = jnp.where(index == place, jnp.int32(table[place]), result)
    return result


def dot(a, b):
    return jnp.dot(a, b, preferred_element_type=jnp.float32)


def body(inv_diag, below, rhs, tile_count, tile_owner, tile_rows, parent_rhs):
    rows = rhs.shape[1]
    piece = rows // (2 * CHAINS)
    tiles = tile_owner.shape[1]
    height = tile_rows.shape[2]
    parent_height = parent_rhs.shape[1]
    fronts = lax.axis_size("front")
    wide = lax.axis_size("wide")
    me = lax.axis_index("front")
    wide_index = lax.axis_index("wide")
    order = ring_order(wide)
    place = lookup([order.index(i) for i in range(wide)], wide_index)
    onward = [(order[i], order[(i + 1) % wide]) for i in range(wide)]
    backward = [(b, a) for a, b in onward]
    from_left = [lookup(order, (place + wide - step) % wide) for step in range(wide)]
    from_right = [lookup(order, (place + step) % wide) for step in range(wide)]

    def part(matrix, index, offset, values):
        columns = lax.dynamic_slice_in_dim(matrix, index * rows + offset, values.shape[0], 1)
        return dot(columns, values)

    def ring_product(matrix, block, aside=None):
        half = rows // 2
        sides = [
            [block[side * half + c * piece:side * half + (c + 1) * piece] for c in range(CHAINS)]
            for side in range(2)
        ]
        total = part(matrix, wide_index, 0, block)
        extra = None
        for step in range(1, wide):
            for chain in range(CHAINS):
                for side, pairs in enumerate((onward, backward)):
                    sides[side][chain] = lax.ppermute(sides[side][chain], "wide", pairs)
            if aside and step == ROUTING_STEPS[0]:
                extra, sides[0][0] = aside(sides[0][0])
            if aside and step == ROUTING_STEPS[1]:
                sides[0][0], extra = lax.optimization_barrier((sides[0][0], extra))
            for side, source in enumerate((from_left[step], from_right[step])):
                values = jnp.concatenate(sides[side], axis=0)
                total = total + part(matrix, source, side * half, values)
        return total.astype(jnp.bfloat16), extra

    swaps = [[(i, i ^ delta) for i in range(fronts)] for delta in range(fronts)]

    def routing(after):
        counts, owners, places, after = lax.optimization_barrier(
            (tile_count, tile_owner, tile_rows, after)
        )
        serial = jnp.arange(tiles, dtype=jnp.int32)
        live_count = jnp.sum(jnp.where(jnp.arange(fronts) == me, counts, 0))
        alive = wide_index * tiles + serial < live_count
        owners = owners[0, :, 0]
        same_owner = owners[:, None] == owners[None, :]
        earlier = serial[None, :] < serial[:, None]
        slot = jnp.sum((same_owner & earlier).astype(jnp.int32), axis=1)
        seat = (owners ^ me) * CAPACITY + slot
        slots = fronts * CAPACITY
        chosen = jnp.arange(slots, dtype=jnp.int32)[:, None] == seat[None, :]
        shifted = jnp.where(alive[:, None], places[0] - parent_height, 0)
        rows_out = parent_height + jnp.sum(jnp.where(chosen[:, :, None], shifted[None], 0), axis=1)
        rows_out = rows_out.reshape(fronts, CAPACITY * height)
        rows_in = [rows_out[0]] + [
            lax.ppermute(rows_out[delta], "front", swaps[delta]) for delta in range(1, fronts)
        ]
        picker = (
            jnp.arange(slots * height, dtype=jnp.int32)[:, None]
            == (seat[:, None] * height + jnp.arange(height, dtype=jnp.int32)[None, :]).reshape(1, -1)
        ).astype(jnp.bfloat16)
        picker = picker.reshape(fronts, CAPACITY * height, tiles * height)
        alive_rows = jnp.broadcast_to(alive[:, None], (tiles, height)).reshape(-1, 1)
        return (rows_in, picker, alive_rows), after

    solved, (rows_in, picker, alive_rows) = ring_product(inv_diag[0], rhs[0], routing)
    numbers = jnp.arange(parent_height, dtype=jnp.int32)[:, None]

    update, _ = ring_product(below[0], solved)
    update = jnp.where(alive_rows, update, jnp.zeros_like(update))
    values_out = [dot(picker[delta], update).astype(jnp.bfloat16) for delta in range(fronts)]
    values_in = [values_out[0]] + [
        lax.ppermute(values_out[delta], "front", swaps[delta]) for delta in range(1, fronts)
    ]
    parent_new = parent_rhs[0].astype(jnp.float32)
    for rows_here, values in zip(rows_in, values_in):
        hits = (numbers == rows_here[None, :]).astype(jnp.bfloat16)
        parent_new = parent_new - dot(hits, values)
    return (solved[None], parent_new[None])


def solution(mesh):
    split = P("front", "wide", None)
    return jax.shard_map(
        body,
        mesh=mesh,
        in_specs=(split, split, split, P(), split, split, split),
        out_specs=(split, split),
        check_vma=False,
    )
```

```python
import jax
import jax.numpy as jnp
from jax import lax
from jax.sharding import PartitionSpec as P

CAPACITY = 2
CHAINS = 2
ROUTING_STEPS = (2, 4)


def ring_order(count):
    if count % 8:
        return list(range(count))
    depth = 4
    columns = count // depth
    walk = [z * columns for z in range(depth)]
    for step, z in enumerate(range(depth - 1, -1, -1)):
        ys = range(1, columns) if step % 2 == 0 else range(columns - 1, 0, -1)
        walk += [z * columns + y for y in ys]
    return walk


def lookup(table, index):
    result = jnp.int32(table[0])
    for place in range(1, len(table)):
        result = jnp.where(index == place, jnp.int32(table[place]), result)
    return result


def dot(a, b):
    return jnp.dot(a, b, preferred_element_type=jnp.float32)


def body(inv_diag, below, rhs, tile_count, tile_owner, tile_rows, parent_rhs):
    rows = rhs.shape[1]
    piece = rows // (2 * CHAINS)
    tiles = tile_owner.shape[1]
    height = tile_rows.shape[2]
    parent_height = parent_rhs.shape[1]
    fronts = lax.axis_size("front")
    wide = lax.axis_size("wide")
    me = lax.axis_index("front")
    wide_index = lax.axis_index("wide")
    order = ring_order(wide)
    place = lookup([order.index(i) for i in range(wide)], wide_index)
    onward = [(order[i], order[(i + 1) % wide]) for i in range(wide)]
    backward = [(b, a) for a, b in onward]
    from_left = [lookup(order, (place + wide - step) % wide) for step in range(wide)]
    from_right = [lookup(order, (place + step) % wide) for step in range(wide)]

    def part(matrix, index, offset, values):
        columns = lax.dynamic_slice_in_dim(matrix, index * rows + offset, values.shape[0], 1)
        return dot(columns, values)

    def ring_product(matrix, block, aside=None):
        half = rows // 2
        sides = [
            [block[side * half + c * piece:side * half + (c + 1) * piece] for c in range(CHAINS)]
            for side in range(2)
        ]
        total = part(matrix, wide_index, 0, block)
        extra = None
        for step in range(1, wide):
            for chain in range(CHAINS):
                for side, pairs in enumerate((onward, backward)):
                    sides[side][chain] = lax.ppermute(sides[side][chain], "wide", pairs)
            if aside and step == ROUTING_STEPS[0]:
                extra, sides[0][0] = aside(sides[0][0])
            if aside and step == ROUTING_STEPS[1]:
                sides[0][0], extra = lax.optimization_barrier((sides[0][0], extra))
            for side, source in enumerate((from_left[step], from_right[step])):
                values = jnp.concatenate(sides[side], axis=0)
                total = total + part(matrix, source, side * half, values)
        return total.astype(jnp.bfloat16), extra

    swaps = [[(i, i ^ delta) for i in range(fronts)] for delta in range(fronts)]

    def routing(after):
        counts, owners, places, after = lax.optimization_barrier(
            (tile_count, tile_owner, tile_rows, after)
        )
        serial = jnp.arange(tiles, dtype=jnp.int32)
        live_count = jnp.sum(jnp.where(jnp.arange(fronts) == me, counts, 0))
        alive = wide_index * tiles + serial < live_count
        owners = owners[0, :, 0]
        same_owner = owners[:, None] == owners[None, :]
        earlier = serial[None, :] < serial[:, None]
        slot = jnp.sum((same_owner & earlier).astype(jnp.int32), axis=1)
        slots = fronts * CAPACITY
        seat = jnp.where(alive, (owners ^ me) * CAPACITY + slot, slots)
        chosen = jnp.arange(slots, dtype=jnp.int32)[:, None] == seat[None, :]
        shifted = places[0] - parent_height
        rows_out = parent_height + jnp.sum(jnp.where(chosen[:, :, None], shifted[None], 0), axis=1)
        rows_out = rows_out.reshape(fronts, CAPACITY * height)
        rows_in = [rows_out[0]] + [
            lax.ppermute(rows_out[delta], "front", swaps[delta]) for delta in range(1, fronts)
        ]
        picker = (
            jnp.arange(slots * height, dtype=jnp.int32)[:, None]
            == (seat[:, None] * height + jnp.arange(height, dtype=jnp.int32)[None, :]).reshape(1, -1)
        ).astype(jnp.bfloat16)
        picker = picker.reshape(fronts, CAPACITY * height, tiles * height)
        return (rows_in, picker), after

    solved, (rows_in, picker) = ring_product(inv_diag[0], rhs[0], routing)
    numbers = jnp.arange(parent_height, dtype=jnp.int32)[:, None]

    update, _ = ring_product(below[0], solved)
    values_out = [dot(picker[delta], update).astype(jnp.bfloat16) for delta in range(fronts)]
    values_in = [values_out[0]] + [
        lax.ppermute(values_out[delta], "front", swaps[delta]) for delta in range(1, fronts)
    ]
    parent_new = parent_rhs[0].astype(jnp.float32)
    for rows_here, values in zip(rows_in, values_in):
        hits = (numbers == rows_here[None, :]).astype(jnp.bfloat16)
        parent_new = parent_new - dot(hits, values)
    return (solved[None], parent_new[None])


def solution(mesh):
    split = P("front", "wide", None)
    return jax.shard_map(
        body,
        mesh=mesh,
        in_specs=(split, split, split, P(), split, split, split),
        out_specs=(split, split),
        check_vma=False,
    )
```

```python
import jax
import jax.numpy as jnp
from jax import lax
from jax.experimental.layout import Layout, with_layout_constraint
from jax.sharding import PartitionSpec as P

CAPACITY = 2
LANES = 128
DEPTH = 4


def row_major(array):
    return with_layout_constraint(array, Layout(major_to_minor=tuple(range(array.ndim))))


def dot(a, b):
    return row_major(jnp.dot(a, b, preferred_element_type=jnp.float32))


def body(inv_diag, below, rhs, tile_count, tile_owner, tile_rows, parent_rhs):
    width = rhs.shape[2]
    rows = rhs.shape[1]
    tiles = tile_owner.shape[1]
    height = tile_rows.shape[2]
    parent_height = parent_rhs.shape[1]
    fronts = lax.axis_size("front")
    wide = lax.axis_size("wide")
    me = lax.axis_index("front")
    wide_index = lax.axis_index("wide")
    depth = DEPTH if wide % DEPTH == 0 else 1
    across = wide // depth
    z, y = wide_index // across, wide_index % across
    z_ring = [(i, (i + across) % wide) for i in range(wide)]
    y_shifts = [
        [(i, i // across * across + (i + shift) % across) for i in range(wide)]
        for shift in range(across)
    ]

    def block_of(step, shift):
        return (z + depth - step) % depth * across + (y + across - shift) % across

    def part(matrix, step, shift, values):
        columns = lax.dynamic_slice_in_dim(matrix, block_of(step, shift) * rows, rows, 1)
        return dot(columns, values)

    def gathered_product(matrix, blocks, later=None, aside=None):
        column_count = len(blocks)
        held_now = list(blocks)
        total = part(matrix, 0, 0, jnp.concatenate(blocks, axis=1))
        waiting = []
        extra = None
        for step in range(depth):
            if step:
                held_now = following
                held_now[0], total, later = lax.optimization_barrier((held_now[0], total, later))
            if aside and step == 1:
                extra, held_now[0] = aside(held_now[0])
            if aside and step == depth - 1:
                held_now[0], extra = lax.optimization_barrier((held_now[0], extra))
            following = [lax.ppermute(b, "wide", z_ring) for b in held_now] if step < depth - 1 else None
            passed = [
                [lax.ppermute(b, "wide", y_shifts[shift]) for b in held_now]
                for shift in range(1, across)
            ]
            if step:
                total = total + part(matrix, step, 0, jnp.concatenate(held_now, axis=1))
            for at, shift, pieces in waiting:
                total = total + part(matrix, at, shift, jnp.concatenate(pieces, axis=1))
            waiting = [(step, shift, passed[shift - 1]) for shift in range(1, across)]
        results = []
        for column in range(column_count):
            piece = total[:, column * LANES:(column + 1) * LANES]
            for at, shift, pieces in waiting:
                piece = piece + part(matrix, at, shift, pieces[column])
            results.append(piece.astype(jnp.bfloat16))
        return results, later, extra

    swaps = [[(i, i ^ delta) for i in range(fronts)] for delta in range(fronts)]

    def routing(after):
        counts, owners, places, after = lax.optimization_barrier(
            (tile_count, tile_owner, tile_rows, after)
        )
        serial = jnp.arange(tiles, dtype=jnp.int32)
        live_count = jnp.sum(jnp.where(jnp.arange(fronts) == me, counts, 0))
        alive = wide_index * tiles + serial < live_count
        owners = owners[0, :, 0]
        same_owner = owners[:, None] == owners[None, :]
        earlier = serial[None, :] < serial[:, None]
        slot = jnp.sum((same_owner & earlier).astype(jnp.int32), axis=1)
        slots = fronts * CAPACITY
        seat = jnp.where(alive, (owners ^ me) * CAPACITY + slot, slots)
        chosen = jnp.arange(slots, dtype=jnp.int32)[:, None] == seat[None, :]
        shifted = places[0] - parent_height
        rows_out = parent_height + jnp.sum(jnp.where(chosen[:, :, None], shifted[None], 0), axis=1)
        rows_out = rows_out.reshape(fronts, CAPACITY * height)
        rows_in = [rows_out[0]] + [
            lax.ppermute(rows_out[delta], "front", swaps[delta]) for delta in range(1, fronts)
        ]
        picker = (
            jnp.arange(slots * height, dtype=jnp.int32)[:, None]
            == (seat[:, None] * height + jnp.arange(height, dtype=jnp.int32)[None, :]).reshape(1, -1)
        ).astype(jnp.bfloat16)
        picker = picker.reshape(fronts, CAPACITY * height, tiles * height)
        return (rows_in, picker), after

    cuts = range(0, width, LANES)
    solved, below_rows, (rows_in, picker) = gathered_product(
        inv_diag[0], [rhs[0][:, c:c + LANES] for c in cuts], below[0], routing
    )
    numbers = jnp.arange(parent_height, dtype=jnp.int32)[:, None]

    updates, _, _ = gathered_product(below_rows, solved)
    results = []
    for c, update in zip(cuts, updates):
        values_out = [dot(picker[delta], update).astype(jnp.bfloat16) for delta in range(fronts)]
        values_in = [values_out[0]] + [
            lax.ppermute(values_out[delta], "front", swaps[delta]) for delta in range(1, fronts)
        ]
        total = parent_rhs[0][:, c:c + LANES].astype(jnp.float32)
        for rows_here, values in zip(rows_in, values_in):
            hits = (numbers == rows_here[None, :]).astype(jnp.bfloat16)
            total = total - dot(hits, values)
        results.append(total)
    return (
        jnp.concatenate(solved, axis=1)[None],
        jnp.concatenate(results, axis=1)[None],
    )


def solution(mesh):
    split = P("front", "wide", None)
    return jax.shard_map(
        body,
        mesh=mesh,
        in_specs=(split, split, split, P(), split, split, split),
        out_specs=(split, split),
        check_vma=False,
    )
```

```python
import jax
import jax.numpy as jnp
from jax import lax
from jax.experimental.layout import Layout, with_layout_constraint
from jax.sharding import PartitionSpec as P

CAPACITY = 2
BASE = 256
LANES = 128
DEPTH = 4


def row_major(array):
    return with_layout_constraint(array, Layout(major_to_minor=tuple(range(array.ndim))))


def dot(a, b):
    return row_major(jnp.dot(a, b, preferred_element_type=jnp.float32))


def body(inv_diag, below, rhs, tile_count, tile_owner, tile_rows, parent_rhs):
    width = rhs.shape[2]
    rows = rhs.shape[1]
    tiles = tile_owner.shape[1]
    height = tile_rows.shape[2]
    parent_height = parent_rhs.shape[1]
    fronts = lax.axis_size("front")
    wide = lax.axis_size("wide")
    me = lax.axis_index("front")
    wide_index = lax.axis_index("wide")
    depth = DEPTH if wide % DEPTH == 0 else 1
    across = wide // depth
    z, y = wide_index // across, wide_index % across
    z_ring = [(i, (i + across) % wide) for i in range(wide)]
    y_shifts = [
        [(i, i // across * across + (i + shift) % across) for i in range(wide)]
        for shift in range(across)
    ]

    def block_of(step, shift):
        return (z + depth - step) % depth * across + (y + across - shift) % across

    def part(matrix, step, shift, values):
        columns = lax.dynamic_slice_in_dim(matrix, block_of(step, shift) * rows, rows, 1)
        return dot(columns, values)

    def gathered_product(matrix, blocks):
        column_count = len(blocks)
        total = part(matrix, 0, 0, jnp.concatenate(blocks, axis=1))
        waiting = []
        following = list(blocks)
        for step in range(depth):
            held_now = following
            if step:
                held_now[0], total = lax.optimization_barrier((held_now[0], total))
            following = [lax.ppermute(b, "wide", z_ring) for b in held_now] if step < depth - 1 else None
            passed = [
                [lax.ppermute(b, "wide", y_shifts[shift]) for b in held_now]
                for shift in range(1, across)
            ]
            if step:
                total = total + part(matrix, step, 0, jnp.concatenate(held_now, axis=1))
            for at, shift, pieces in waiting:
                total = total + part(matrix, at, shift, jnp.concatenate(pieces, axis=1))
            waiting = [(step, shift, passed[shift - 1]) for shift in range(1, across)]
        results = []
        for column in range(column_count):
            piece = total[:, column * LANES:(column + 1) * LANES]
            for at, shift, pieces in waiting:
                piece = piece + part(matrix, at, shift, pieces[column])
            results.append(piece.astype(jnp.bfloat16))
        return results

    swaps = [[(i, i ^ delta) for i in range(fronts)] for delta in range(fronts)]
    serial = jnp.arange(tiles, dtype=jnp.int32)
    live_count = jnp.sum(jnp.where(jnp.arange(fronts) == me, tile_count, 0))
    alive = wide_index * tiles + serial < live_count
    owners = tile_owner[0, :, 0]
    same_owner = owners[:, None] == owners[None, :]
    earlier = serial[None, :] < serial[:, None]
    slot = jnp.sum((same_owner & earlier).astype(jnp.int32), axis=1)
    slots = fronts * CAPACITY
    seat = jnp.where(alive, (owners ^ me) * CAPACITY + slot, slots)
    chosen = jnp.arange(slots, dtype=jnp.int32)[:, None] == seat[None, :]
    shifted = tile_rows[0] - parent_height
    rows_out = parent_height + jnp.sum(jnp.where(chosen[:, :, None], shifted[None], 0), axis=1)
    digits = jnp.stack(
        [
            (rows_out // BASE).reshape(fronts, CAPACITY, height),
            (rows_out % BASE).reshape(fronts, CAPACITY, height),
        ],
        axis=1,
    ).astype(jnp.bfloat16).reshape(fronts, 2 * CAPACITY, height)
    digits = jnp.pad(digits, ((0, 0), (0, 16 - 2 * CAPACITY), (0, 0)))
    picker = (
        jnp.arange(slots * height, dtype=jnp.int32)[:, None]
        == (seat[:, None] * height + jnp.arange(height, dtype=jnp.int32)[None, :]).reshape(1, -1)
    ).astype(jnp.bfloat16)
    picker = picker.reshape(fronts, CAPACITY * height, tiles * height)

    cuts = range(0, width, LANES)
    solved = gathered_product(inv_diag[0], [rhs[0][:, c:c + LANES] for c in cuts])
    numbers = jnp.arange(parent_height, dtype=jnp.int32)[:, None]

    updates = gathered_product(below[0], solved)
    tall = CAPACITY * height
    hits = [None] * fronts
    results = []
    for c, update in zip(cuts, updates):
        total = parent_rhs[0][:, c:c + LANES].astype(jnp.float32)
        for delta in range(fronts):
            values = dot(picker[delta], update).astype(jnp.bfloat16)
            if c == 0:
                values = jnp.concatenate([values, digits[delta]], axis=0)
            if delta:
                values = lax.ppermute(values, "front", swaps[delta])
            if c == 0:
                pair = values[tall:tall + 2 * CAPACITY].astype(jnp.float32).astype(jnp.int32)
                places = (pair[:CAPACITY] * BASE + pair[CAPACITY:]).reshape(1, -1)
                hits[delta] = (numbers == places).astype(jnp.bfloat16)
            total = total - dot(hits[delta], values[:tall])
        results.append(total)
    return (
        jnp.concatenate(solved, axis=1)[None],
        jnp.concatenate(results, axis=1)[None],
    )


def solution(mesh):
    split = P("front", "wide", None)
    return jax.shard_map(
        body,
        mesh=mesh,
        in_specs=(split, split, split, P(), split, split, split),
        out_specs=(split, split),
        check_vma=False,
    )
```

```python
import jax
import jax.numpy as jnp
from jax import lax
from jax.experimental.layout import Layout, with_layout_constraint
from jax.sharding import PartitionSpec as P

CAPACITY = 2
BASE = 256
LANES = 128
DEPTH = 4


def row_major(array):
    return with_layout_constraint(array, Layout(major_to_minor=tuple(range(array.ndim))))


def dot(a, b):
    return row_major(jnp.dot(a, b, preferred_element_type=jnp.float32))


def body(inv_diag, below, rhs, tile_count, tile_owner, tile_rows, parent_rhs):
    width = rhs.shape[2]
    rows = rhs.shape[1]
    tiles = tile_owner.shape[1]
    height = tile_rows.shape[2]
    parent_height = parent_rhs.shape[1]
    fronts = lax.axis_size("front")
    wide = lax.axis_size("wide")
    me = lax.axis_index("front")
    wide_index = lax.axis_index("wide")
    depth = DEPTH if wide % DEPTH == 0 else 1
    across = wide // depth
    z, y = wide_index // across, wide_index % across
    z_ring = [(i, (i + across) % wide) for i in range(wide)]
    y_shifts = [
        [(i, i // across * across + (i + shift) % across) for i in range(wide)]
        for shift in range(across)
    ]

    def block_of(step, shift):
        return (z + depth - step) % depth * across + (y + across - shift) % across

    def part(matrix, step, shift, values):
        columns = lax.dynamic_slice_in_dim(matrix, block_of(step, shift) * rows, rows, 1)
        return dot(columns, values)

    def gathered_product(matrix, blocks, paired):
        column_count = len(blocks)
        total = part(matrix, 0, 0, jnp.concatenate(blocks, axis=1))
        waiting = []
        following = list(blocks)
        for step in range(depth):
            held_now = following
            if step:
                held_now[0], total = lax.optimization_barrier((held_now[0], total))
                for column in paired[step]:
                    last = [pieces[column] for _, _, pieces in waiting]
                    held_now[column], last = lax.optimization_barrier((held_now[column], last))
                    for entry, piece in zip(waiting, last):
                        entry[2][column] = piece
            following = [lax.ppermute(b, "wide", z_ring) for b in held_now] if step < depth - 1 else None
            passed = [
                [lax.ppermute(b, "wide", y_shifts[shift]) for b in held_now]
                for shift in range(1, across)
            ]
            if step:
                total = total + part(matrix, step, 0, jnp.concatenate(held_now, axis=1))
            for at, shift, pieces in waiting:
                total = total + part(matrix, at, shift, jnp.concatenate(pieces, axis=1))
            waiting = [(step, shift, passed[shift - 1]) for shift in range(1, across)]
        results = []
        for column in range(column_count):
            piece = total[:, column * LANES:(column + 1) * LANES]
            for at, shift, pieces in waiting:
                piece = piece + part(matrix, at, shift, pieces[column])
            results.append(piece.astype(jnp.bfloat16))
        return results

    swaps = [[(i, i ^ delta) for i in range(fronts)] for delta in range(fronts)]
    serial = jnp.arange(tiles, dtype=jnp.int32)
    live_count = jnp.sum(jnp.where(jnp.arange(fronts) == me, tile_count, 0))
    alive = wide_index * tiles + serial < live_count
    owners = tile_owner[0, :, 0]
    same_owner = owners[:, None] == owners[None, :]
    earlier = serial[None, :] < serial[:, None]
    slot = jnp.sum((same_owner & earlier).astype(jnp.int32), axis=1)
    slots = fronts * CAPACITY
    seat = jnp.where(alive, (owners ^ me) * CAPACITY + slot, slots)
    chosen = jnp.arange(slots, dtype=jnp.int32)[:, None] == seat[None, :]
    shifted = tile_rows[0] - parent_height
    rows_out = parent_height + jnp.sum(jnp.where(chosen[:, :, None], shifted[None], 0), axis=1)
    digits = jnp.stack(
        [
            (rows_out // BASE).reshape(fronts, CAPACITY, height),
            (rows_out % BASE).reshape(fronts, CAPACITY, height),
        ],
        axis=1,
    ).astype(jnp.bfloat16).reshape(fronts, 2 * CAPACITY, height)
    digits = jnp.pad(digits, ((0, 0), (0, 16 - 2 * CAPACITY), (0, 0)))
    picker = (
        jnp.arange(slots * height, dtype=jnp.int32)[:, None]
        == (seat[:, None] * height + jnp.arange(height, dtype=jnp.int32)[None, :]).reshape(1, -1)
    ).astype(jnp.bfloat16)
    picker = picker.reshape(fronts, CAPACITY * height, tiles * height)

    cuts = range(0, width, LANES)
    solved = gathered_product(inv_diag[0], [rhs[0][:, c:c + LANES] for c in cuts], ((), (0, 1), (0, 1), ()))
    numbers = jnp.arange(parent_height, dtype=jnp.int32)[:, None]

    updates = gathered_product(below[0], solved, ((), (0, 1), (0, 1), (0,)))
    tall = CAPACITY * height
    hits = [None] * fronts
    results = []
    for c, update in zip(cuts, updates):
        total = parent_rhs[0][:, c:c + LANES].astype(jnp.float32)
        for delta in range(fronts):
            values = dot(picker[delta], update).astype(jnp.bfloat16)
            if c == 0:
                values = jnp.concatenate([values, digits[delta]], axis=0)
            if delta:
                values = lax.ppermute(values, "front", swaps[delta])
            if c == 0:
                pair = values[tall:tall + 2 * CAPACITY].astype(jnp.float32).astype(jnp.int32)
                places = (pair[:CAPACITY] * BASE + pair[CAPACITY:]).reshape(1, -1)
                hits[delta] = (numbers == places).astype(jnp.bfloat16)
            total = total - dot(hits[delta], values[:tall])
        results.append(total)
    return (
        jnp.concatenate(solved, axis=1)[None],
        jnp.concatenate(results, axis=1)[None],
    )


def solution(mesh):
    split = P("front", "wide", None)
    return jax.shard_map(
        body,
        mesh=mesh,
        in_specs=(split, split, split, P(), split, split, split),
        out_specs=(split, split),
        check_vma=False,
    )
```

```python
import jax
import jax.numpy as jnp
from jax import lax
from jax.experimental.layout import Layout, with_layout_constraint
from jax.sharding import PartitionSpec as P

CAPACITY = 2
BASE = 256
LANES = 128
DEPTH = 4


def row_major(array):
    return with_layout_constraint(array, Layout(major_to_minor=tuple(range(array.ndim))))


def dot(a, b):
    return row_major(jnp.dot(a, b, preferred_element_type=jnp.float32))


def body(inv_diag, below, rhs, tile_count, tile_owner, tile_rows, parent_rhs):
    width = rhs.shape[2]
    rows = rhs.shape[1]
    tiles = tile_owner.shape[1]
    height = tile_rows.shape[2]
    parent_height = parent_rhs.shape[1]
    fronts = lax.axis_size("front")
    wide = lax.axis_size("wide")
    me = lax.axis_index("front")
    wide_index = lax.axis_index("wide")
    depth = DEPTH if wide % DEPTH == 0 else 1
    across = wide // depth
    z, y = wide_index // across, wide_index % across
    z_ring = [(i, (i + across) % wide) for i in range(wide)]
    y_shifts = [
        [(i, i // across * across + (i + shift) % across) for i in range(wide)]
        for shift in range(across)
    ]

    def block_of(step, shift):
        return (z + depth - step) % depth * across + (y + across - shift) % across

    def part(matrix, step, shift, values):
        columns = lax.dynamic_slice_in_dim(matrix, block_of(step, shift) * rows, rows, 1)
        return dot(columns, values)

    def gathered_product(matrix, blocks, paired):
        column_count = len(blocks)
        total = part(matrix, 0, 0, jnp.concatenate(blocks, axis=1))
        waiting = []
        following = list(blocks)
        for step in range(depth):
            held_now = following
            if step:
                held_now[0], total = lax.optimization_barrier((held_now[0], total))
                for column in paired[step]:
                    last = [pieces[column] for _, _, pieces in waiting]
                    held_now[column], last = lax.optimization_barrier((held_now[column], last))
                    for entry, piece in zip(waiting, last):
                        entry[2][column] = piece
            following = [lax.ppermute(b, "wide", z_ring) for b in held_now] if step < depth - 1 else None
            passed = [
                [lax.ppermute(b, "wide", y_shifts[shift]) for b in held_now]
                for shift in range(1, across)
            ]
            if step == depth - 1:
                for entry, (_, _, pieces) in zip(passed, waiting):
                    entry[0] = lax.ppermute(pieces[0], "wide", z_ring)
            if step:
                total = total + part(matrix, step, 0, jnp.concatenate(held_now, axis=1))
            for at, shift, pieces in waiting:
                total = total + part(matrix, at, shift, jnp.concatenate(pieces, axis=1))
            waiting = [(step, shift, passed[shift - 1]) for shift in range(1, across)]
        results = []
        for column in range(column_count):
            piece = total[:, column * LANES:(column + 1) * LANES]
            for at, shift, pieces in waiting:
                piece = piece + part(matrix, at, shift, pieces[column])
            results.append(piece.astype(jnp.bfloat16))
        return results

    swaps = [[(i, i ^ delta) for i in range(fronts)] for delta in range(fronts)]
    serial = jnp.arange(tiles, dtype=jnp.int32)
    live_count = jnp.sum(jnp.where(jnp.arange(fronts) == me, tile_count, 0))
    alive = wide_index * tiles + serial < live_count
    owners = tile_owner[0, :, 0]
    same_owner = owners[:, None] == owners[None, :]
    earlier = serial[None, :] < serial[:, None]
    slot = jnp.sum((same_owner & earlier).astype(jnp.int32), axis=1)
    slots = fronts * CAPACITY
    seat = jnp.where(alive, (owners ^ me) * CAPACITY + slot, slots)
    chosen = jnp.arange(slots, dtype=jnp.int32)[:, None] == seat[None, :]
    shifted = tile_rows[0] - parent_height
    rows_out = parent_height + jnp.sum(jnp.where(chosen[:, :, None], shifted[None], 0), axis=1)
    digits = jnp.stack(
        [
            (rows_out // BASE).reshape(fronts, CAPACITY, height),
            (rows_out % BASE).reshape(fronts, CAPACITY, height),
        ],
        axis=1,
    ).astype(jnp.bfloat16).reshape(fronts, 2 * CAPACITY, height)
    digits = jnp.pad(digits, ((0, 0), (0, 16 - 2 * CAPACITY), (0, 0)))
    picker = (
        jnp.arange(slots * height, dtype=jnp.int32)[:, None]
        == (seat[:, None] * height + jnp.arange(height, dtype=jnp.int32)[None, :]).reshape(1, -1)
    ).astype(jnp.bfloat16)
    picker = picker.reshape(fronts, CAPACITY * height, tiles * height)

    cuts = range(0, width, LANES)
    solved = gathered_product(inv_diag[0], [rhs[0][:, c:c + LANES] for c in cuts], ((), (0, 1), (0, 1), ()))
    numbers = jnp.arange(parent_height, dtype=jnp.int32)[:, None]

    updates = gathered_product(below[0], solved, ((), (0, 1), (0, 1), (0,)))
    tall = CAPACITY * height
    hits = [None] * fronts
    results = []
    for c, update in zip(cuts, updates):
        total = parent_rhs[0][:, c:c + LANES].astype(jnp.float32)
        for delta in range(fronts):
            values = dot(picker[delta], update).astype(jnp.bfloat16)
            if c == 0:
                values = jnp.concatenate([values, digits[delta]], axis=0)
            if delta:
                values = lax.ppermute(values, "front", swaps[delta])
            if c == 0:
                pair = values[tall:tall + 2 * CAPACITY].astype(jnp.float32).astype(jnp.int32)
                places = (pair[:CAPACITY] * BASE + pair[CAPACITY:]).reshape(1, -1)
                hits[delta] = (numbers == places).astype(jnp.bfloat16)
            total = total - dot(hits[delta], values[:tall])
        results.append(total)
    return (
        jnp.concatenate(solved, axis=1)[None],
        jnp.concatenate(results, axis=1)[None],
    )


def solution(mesh):
    split = P("front", "wide", None)
    return jax.shard_map(
        body,
        mesh=mesh,
        in_specs=(split, split, split, P(), split, split, split),
        out_specs=(split, split),
        check_vma=False,
    )
```

```python
import jax
import jax.numpy as jnp
from jax import lax
from jax.experimental.layout import Layout, with_layout_constraint
from jax.sharding import PartitionSpec as P

CAPACITY = 2
BASE = 256
LANES = 128
DEPTH = 4


def row_major(array):
    return with_layout_constraint(array, Layout(major_to_minor=tuple(range(array.ndim))))


def dot(a, b):
    return row_major(jnp.dot(a, b, preferred_element_type=jnp.float32))


def body(inv_diag, below, rhs, tile_count, tile_owner, tile_rows, parent_rhs):
    width = rhs.shape[2]
    rows = rhs.shape[1]
    tiles = tile_owner.shape[1]
    height = tile_rows.shape[2]
    parent_height = parent_rhs.shape[1]
    fronts = lax.axis_size("front")
    wide = lax.axis_size("wide")
    me = lax.axis_index("front")
    wide_index = lax.axis_index("wide")
    depth = DEPTH if wide % DEPTH == 0 else 1
    across = wide // depth
    z, y = wide_index // across, wide_index % across
    z_ring = [(i, (i + across) % wide) for i in range(wide)]
    y_shifts = [
        [(i, i // across * across + (i + shift) % across) for i in range(wide)]
        for shift in range(across)
    ]

    def block_of(step, shift):
        return (z + depth - step) % depth * across + (y + across - shift) % across

    def part(matrix, step, shift, values):
        columns = lax.dynamic_slice_in_dim(matrix, block_of(step, shift) * rows, rows, 1)
        return dot(columns, values)

    def gathered_product(matrix, blocks, paired):
        column_count = len(blocks)
        total = part(matrix, 0, 0, jnp.concatenate(blocks, axis=1))
        waiting = []
        following = list(blocks)
        for step in range(depth):
            held_now = following
            if step:
                held_now[0], total = lax.optimization_barrier((held_now[0], total))
                for column in paired[step]:
                    last = [pieces[column] for _, _, pieces in waiting]
                    held_now[column], last = lax.optimization_barrier((held_now[column], last))
                    for entry, piece in zip(waiting, last):
                        entry[2][column] = piece
            following = [lax.ppermute(b, "wide", z_ring) for b in held_now] if step < depth - 1 else None
            passed = [
                [lax.ppermute(b, "wide", y_shifts[shift]) for b in held_now]
                for shift in range(1, across)
            ]
            if step == depth - 1:
                for entry, (_, _, pieces) in zip(passed, waiting):
                    entry[-1] = lax.ppermute(pieces[-1], "wide", z_ring)
            if step:
                total = total + part(matrix, step, 0, jnp.concatenate(held_now, axis=1))
            for at, shift, pieces in waiting:
                total = total + part(matrix, at, shift, jnp.concatenate(pieces, axis=1))
            waiting = [(step, shift, passed[shift - 1]) for shift in range(1, across)]
        results = []
        for column in range(column_count):
            piece = total[:, column * LANES:(column + 1) * LANES]
            for at, shift, pieces in waiting:
                piece = piece + part(matrix, at, shift, pieces[column])
            results.append(piece.astype(jnp.bfloat16))
        return results

    swaps = [[(i, i ^ delta) for i in range(fronts)] for delta in range(fronts)]
    serial = jnp.arange(tiles, dtype=jnp.int32)
    live_count = jnp.sum(jnp.where(jnp.arange(fronts) == me, tile_count, 0))
    alive = wide_index * tiles + serial < live_count
    owners = tile_owner[0, :, 0]
    same_owner = owners[:, None] == owners[None, :]
    earlier = serial[None, :] < serial[:, None]
    slot = jnp.sum((same_owner & earlier).astype(jnp.int32), axis=1)
    slots = fronts * CAPACITY
    seat = jnp.where(alive, (owners ^ me) * CAPACITY + slot, slots)
    chosen = jnp.arange(slots, dtype=jnp.int32)[:, None] == seat[None, :]
    shifted = tile_rows[0] - parent_height
    rows_out = parent_height + jnp.sum(jnp.where(chosen[:, :, None], shifted[None], 0), axis=1)
    digits = jnp.stack(
        [
            (rows_out // BASE).reshape(fronts, CAPACITY, height),
            (rows_out % BASE).reshape(fronts, CAPACITY, height),
        ],
        axis=1,
    ).astype(jnp.bfloat16).reshape(fronts, 2 * CAPACITY, height)
    digits = jnp.pad(digits, ((0, 0), (0, 16 - 2 * CAPACITY), (0, 0)))
    picker = (
        jnp.arange(slots * height, dtype=jnp.int32)[:, None]
        == (seat[:, None] * height + jnp.arange(height, dtype=jnp.int32)[None, :]).reshape(1, -1)
    ).astype(jnp.bfloat16)
    picker = picker.reshape(fronts, CAPACITY * height, tiles * height)

    cuts = range(0, width, LANES)
    solved = gathered_product(inv_diag[0], [rhs[0][:, c:c + LANES] for c in cuts], ((), (0, 1), (0, 1), ()))
    numbers = jnp.arange(parent_height, dtype=jnp.int32)[:, None]

    updates = gathered_product(below[0], solved, ((), (0, 1), (0, 1), (0,)))
    tall = CAPACITY * height
    hits = [None] * fronts
    results = []
    for c, update in zip(cuts, updates):
        total = parent_rhs[0][:, c:c + LANES].astype(jnp.float32)
        for delta in range(fronts):
            values = dot(picker[delta], update).astype(jnp.bfloat16)
            if c == 0:
                values = jnp.concatenate([values, digits[delta]], axis=0)
            if delta:
                values = lax.ppermute(values, "front", swaps[delta])
            if c == 0:
                pair = values[tall:tall + 2 * CAPACITY].astype(jnp.float32).astype(jnp.int32)
                places = (pair[:CAPACITY] * BASE + pair[CAPACITY:]).reshape(1, -1)
                hits[delta] = (numbers == places).astype(jnp.bfloat16)
            total = total - dot(hits[delta], values[:tall])
        results.append(total)
    return (
        jnp.concatenate(solved, axis=1)[None],
        jnp.concatenate(results, axis=1)[None],
    )


def solution(mesh):
    split = P("front", "wide", None)
    return jax.shard_map(
        body,
        mesh=mesh,
        in_specs=(split, split, split, P(), split, split, split),
        out_specs=(split, split),
        check_vma=False,
    )
```

```python
import jax
import jax.numpy as jnp
from jax import lax
from jax.experimental.layout import Layout, with_layout_constraint
from jax.sharding import PartitionSpec as P

CAPACITY = 2
BASE = 256
LANES = 128
DEPTH = 4


def row_major(array):
    return with_layout_constraint(array, Layout(major_to_minor=tuple(range(array.ndim))))


def dot(a, b):
    return row_major(jnp.dot(a, b, preferred_element_type=jnp.float32))


def body(inv_diag, below, rhs, tile_count, tile_owner, tile_rows, parent_rhs):
    width = rhs.shape[2]
    rows = rhs.shape[1]
    tiles = tile_owner.shape[1]
    height = tile_rows.shape[2]
    parent_height = parent_rhs.shape[1]
    fronts = lax.axis_size("front")
    wide = lax.axis_size("wide")
    me = lax.axis_index("front")
    wide_index = lax.axis_index("wide")
    depth = DEPTH if wide % DEPTH == 0 else 1
    across = wide // depth
    z, y = wide_index // across, wide_index % across
    z_ring = [(i, (i + across) % wide) for i in range(wide)]
    y_shifts = [
        [(i, i // across * across + (i + shift) % across) for i in range(wide)]
        for shift in range(across)
    ]

    def block_of(step, shift):
        return (z + depth - step) % depth * across + (y + across - shift) % across

    def part(matrix, step, shift, values):
        columns = lax.dynamic_slice_in_dim(matrix, block_of(step, shift) * rows, rows, 1)
        return dot(columns, values)

    def gathered_product(matrix, blocks, paired, finish=None):
        column_count = len(blocks)
        total = part(matrix, 0, 0, jnp.concatenate(blocks, axis=1))
        waiting = []
        following = list(blocks)
        for step in range(depth):
            held_now = following
            if step:
                held_now[0], total = lax.optimization_barrier((held_now[0], total))
                for column in paired[step]:
                    last = [pieces[column] for _, _, pieces in waiting]
                    held_now[column], last = lax.optimization_barrier((held_now[column], last))
                    for entry, piece in zip(waiting, last):
                        entry[2][column] = piece
            following = [lax.ppermute(b, "wide", z_ring) for b in held_now] if step < depth - 1 else None
            passed = [
                [lax.ppermute(b, "wide", y_shifts[shift]) for b in held_now]
                for shift in range(1, across)
            ]
            if step == depth - 1:
                for entry, (_, _, pieces) in zip(passed, waiting):
                    entry[-1] = lax.ppermute(pieces[-1], "wide", z_ring)
            if step:
                total = total + part(matrix, step, 0, jnp.concatenate(held_now, axis=1))
            for at, shift, pieces in waiting:
                total = total + part(matrix, at, shift, jnp.concatenate(pieces, axis=1))
            waiting = [(step, shift, passed[shift - 1]) for shift in range(1, across)]
        results = []
        for column in range(column_count):
            piece = total[:, column * LANES:(column + 1) * LANES]
            last = [pieces[column] for _, _, pieces in waiting]
            for (at, shift, _), values in zip(waiting, last):
                piece = piece + part(matrix, at, shift, values)
            piece = piece.astype(jnp.bfloat16)
            if finish and column:
                piece, results[-1] = lax.optimization_barrier((piece, results[-1]))
            results.append(finish(column, piece) if finish else piece)
        return results

    swaps = [[(i, i ^ delta) for i in range(fronts)] for delta in range(fronts)]
    serial = jnp.arange(tiles, dtype=jnp.int32)
    live_count = jnp.sum(jnp.where(jnp.arange(fronts) == me, tile_count, 0))
    alive = wide_index * tiles + serial < live_count
    owners = tile_owner[0, :, 0]
    same_owner = owners[:, None] == owners[None, :]
    earlier = serial[None, :] < serial[:, None]
    slot = jnp.sum((same_owner & earlier).astype(jnp.int32), axis=1)
    slots = fronts * CAPACITY
    seat = jnp.where(alive, (owners ^ me) * CAPACITY + slot, slots)
    chosen = jnp.arange(slots, dtype=jnp.int32)[:, None] == seat[None, :]
    shifted = tile_rows[0] - parent_height
    rows_out = parent_height + jnp.sum(jnp.where(chosen[:, :, None], shifted[None], 0), axis=1)
    digits = jnp.stack(
        [
            (rows_out // BASE).reshape(fronts, CAPACITY, height),
            (rows_out % BASE).reshape(fronts, CAPACITY, height),
        ],
        axis=1,
    ).astype(jnp.bfloat16).reshape(fronts, 2 * CAPACITY, height)
    digits = jnp.pad(digits, ((0, 0), (0, 16 - 2 * CAPACITY), (0, 0)))
    picker = (
        jnp.arange(slots * height, dtype=jnp.int32)[:, None]
        == (seat[:, None] * height + jnp.arange(height, dtype=jnp.int32)[None, :]).reshape(1, -1)
    ).astype(jnp.bfloat16)
    picker = picker.reshape(fronts, CAPACITY * height, tiles * height)

    cuts = range(0, width, LANES)
    solved = gathered_product(inv_diag[0], [rhs[0][:, c:c + LANES] for c in cuts], ((), (0, 1), (0, 1), ()))
    numbers = jnp.arange(parent_height, dtype=jnp.int32)[:, None]

    tall = CAPACITY * height

    def exchanged(column, update):
        arrived = []
        for delta in range(fronts):
            values = dot(picker[delta], update).astype(jnp.bfloat16)
            if column == 0:
                values = jnp.concatenate([values, digits[delta]], axis=0)
            arrived.append(lax.ppermute(values, "front", swaps[delta]) if delta else values)
        return arrived

    arrivals = gathered_product(below[0], solved, ((), (0, 1), (0, 1), (0,)), exchanged)
    hits = []
    for values in arrivals[0]:
        pair = values[tall:tall + 2 * CAPACITY].astype(jnp.float32).astype(jnp.int32)
        places = (pair[:CAPACITY] * BASE + pair[CAPACITY:]).reshape(1, -1)
        hits.append((numbers == places).astype(jnp.bfloat16))
    results = []
    for c, arrived in zip(cuts, arrivals):
        total = parent_rhs[0][:, c:c + LANES].astype(jnp.float32)
        for hit, values in zip(hits, arrived):
            total = total - dot(hit, values[:tall])
        results.append(total)
    return (
        jnp.concatenate(solved, axis=1)[None],
        jnp.concatenate(results, axis=1)[None],
    )


def solution(mesh):
    split = P("front", "wide", None)
    return jax.shard_map(
        body,
        mesh=mesh,
        in_specs=(split, split, split, P(), split, split, split),
        out_specs=(split, split),
        check_vma=False,
    )
```
